32 devices in a mesh: rep: 2 (over y), col: 16 (over z, x, core).
Axes of the slice: x: 2, y: 2, z: 4, core: 2. Of those that a mesh axis runs over, the one named last changes fastest.
Arguments:
- alignment: bfloat16 [64, 32, 768], P('rep', 'col'), parts along dimension 0, may hold values from -4 to 4
- norm_gain: bfloat16 [768], replicated, may hold values from 0.099609375 to 1.8984375
- norm_bias: bfloat16 [768], replicated, may hold values from -3 to 3
- w_query: bfloat16 [768, 768], replicated, may hold values from -1 to 1
- w_key: bfloat16 [768, 768], replicated, may hold values from -1 to 1
- w_value: bfloat16 [768, 768], replicated, may hold values from -0.21875 to 0.21875
- w_out: bfloat16 [768, 768], replicated, may hold values from -0.21875 to 0.21875
Outputs:
- update: bfloat16 [64, 32, 768], P('rep', 'col'), parts along dimension 0
The draws below stay inside these ranges and needn't reach their ends.
There are 2 independent parts, one for each index of `rep`. The reference program is written for one: setup_inputs(seed, part) draws one part's arguments, and reference() takes and returns one part's arrays. A program takes and returns all parts, laid end to end along the dimension named above; an argument that names none is the same for every part. Nothing has to cross between parts.
All inputs are finite; a program needn't handle non-finite values.
Results may differ from the reference program's by a relative error of at most 0.004.
The reference program's roundings to bfloat16 on the way count: a program that leaves them out, or rounds other values in their place, can miss the bound.
Values may be sent and summed in bfloat16 or wider, within the bound.
A program may use at most 64 MiB of HBM per device.

```python
import math
import jax
import jax.numpy as jnp
from jax import lax

D = 768
HEADS = 12
DH = 64
SEQ_DEV = 2
SEQS = 32
COLS = 32


def draw_alignment(key, part):
    result = jnp.clip(jax.random.normal(jax.random.fold_in(key, 1), (SEQS, COLS, D), jnp.float32), -4.0, 4.0)
    return result.astype(jnp.bfloat16)


def query_key_pair(key):
    key_draw = jnp.clip(jax.random.normal(jax.random.fold_in(key, 101), (D, D), jnp.float32), -4.0, 4.0) * D ** (-0.5)
    noise = jnp.clip(jax.random.normal(jax.random.fold_in(key, 102), (D, D), jnp.float32), -4.0, 4.0) * D ** (-0.5)
    query_draw = noise
    return (query_draw, key_draw)


def draw_w_query(key, part):
    return query_key_pair(key)[0].astype(jnp.bfloat16)


def draw_w_key(key, part):
    return query_key_pair(key)[1].astype(jnp.bfloat16)


def normal_values(own_key, extent, scale, limit, held_as=jnp.bfloat16):
    values = jax.random.normal(own_key, extent, jnp.float32) * scale
    return jnp.minimum(jnp.maximum(values, -limit), limit).astype(held_as)


def setup_inputs(seed: int = 0, part: int = 0) -> dict:
    splits = jax.random.split(jax.random.key(seed), 8)
    part_keys = jax.random.split(jax.random.fold_in(splits[7], part), 8)
    return {
        "alignment": draw_alignment(jax.random.fold_in(jax.random.fold_in(splits[7], part), 71), part),
        "norm_gain": jnp.clip(1.0 + 0.18 * jax.random.normal(splits[1], (D,), jnp.float32), 0.099609375, 1.8984375).astype(jnp.bfloat16),
        "norm_bias": normal_values(splits[2], (D,), 0.5, 3.0),
        "w_query": draw_w_query(jax.random.fold_in(splits[7], 71), part),
        "w_key": draw_w_key(jax.random.fold_in(splits[7], 71), part),
        "w_value": normal_values(splits[5], (D, D), D ** -0.5, 0.21875),
        "w_out": normal_values(splits[6], (D, D), D ** -0.5, 0.21875),
    }


def normalize(tokens, norm_gain, norm_bias):
    values_f = tokens.astype(jnp.float32)
    center = lax.optimization_barrier(jnp.mean(values_f, axis=-1, keepdims=True))
    spread = lax.optimization_barrier(jnp.mean((values_f - center) ** 2, axis=-1, keepdims=True))
    scaled = (values_f - center) * lax.rsqrt(spread + 1e-05)
    return (scaled * norm_gain.astype(jnp.float32) + norm_bias.astype(jnp.float32)).astype(jnp.bfloat16)

def project_heads(normed_flat, weight, factor, shape_out):
    product = jnp.dot(normed_flat, weight, preferred_element_type=jnp.float32) * factor
    return product.astype(jnp.bfloat16).reshape(shape_out)

def reference(alignment, norm_gain, norm_bias, w_query, w_key, w_value, w_out):
    blocks = alignment.reshape(SEQ_DEV, SEQS // SEQ_DEV, COLS, D)
    head_shape = (SEQS // SEQ_DEV, COLS, HEADS, DH)
    query_factor = 1.0 / math.sqrt(DH * SEQS)

    def logit_step(running, block):
        normed_flat = normalize(block, norm_gain, norm_bias).reshape(-1, D)
        queries = project_heads(normed_flat, w_query, query_factor, head_shape)
        key_rows = project_heads(normed_flat, w_key, 1.0, head_shape)
        partial_sum = jnp.einsum('sihd,sjhd->ihj', queries.astype(jnp.float32), key_rows.astype(jnp.float32), precision=lax.Precision.HIGHEST)
        return (running + partial_sum, None)
    logits, _ = lax.scan(logit_step, jnp.zeros((COLS, HEADS, COLS), jnp.float32), blocks)
    highest = lax.optimization_barrier(jnp.max(logits, axis=-1, keepdims=True))
    expo = jnp.exp(logits - highest)
    weights = (expo / lax.optimization_barrier(jnp.sum(expo, axis=-1, keepdims=True))).astype(jnp.bfloat16)

    def update_block(block):
        normed_flat = normalize(block, norm_gain, norm_bias).reshape(-1, D)
        value_rows = project_heads(normed_flat, w_value, 1.0, head_shape)
        mixed = jnp.einsum('ihj,sjhd->sihd', weights.astype(jnp.float32), value_rows.astype(jnp.float32), precision=lax.Precision.HIGHEST).astype(jnp.bfloat16).reshape(-1, D)
        result = jnp.dot(mixed, w_out, preferred_element_type=jnp.float32).astype(jnp.bfloat16)
        return result.reshape(SEQS // SEQ_DEV, COLS, D)
    updated = lax.map(update_block, blocks)
    return updated.reshape(SEQS, COLS, D)
```

```python
import functools
import math

import jax
import jax.numpy as jnp
from jax import lax
from jax.experimental import pallas as pl
from jax.experimental.pallas import tpu as pltpu
from jax.sharding import PartitionSpec as P

HEADS = 12
MESH = pl.DeviceIdType.MESH


def each(count, body):
    if count <= 16:
        for k in range(count):
            body(k)
    else:
        lax.fori_loop(0, count, lambda k, c: (body(k), c)[1], 0)


def scatter_rows(n, cd, source, put):
    if n <= 16:
        for p in range(n):
            put(p, source[p * cd : (p + 1) * cd, :])
        return
    per = max(8 // cd, 1)

    def body(q):
        tile = source[pl.ds(pl.multiple_of(q * per * cd, per * cd), per * cd), :]
        for k in range(per):
            put(q * per + k, tile[k * cd : (k + 1) * cd, :])

    each(n // per, body)


def gather_rows(n, cd, take, target):
    if n <= 16:
        for p in range(n):
            target[p * cd : (p + 1) * cd, :] = take(p)
        return
    per = max(8 // cd, 1)

    def body(q):
        tile = jnp.concatenate([take(q * per + k) for k in range(per)], axis=0)
        target[pl.ds(pl.multiple_of(q * per * cd, per * cd), per * cd), :] = tile

    each(n // per, body)


def drain(like, sem):
    pltpu.make_async_copy(like, like, sem).wait()


def kernel(
    n, x, gain, bias, wq, wk, wv, wo, out,
    toks, rows, gb, bb, ws, lg, lg_send, lg_recv, wt_all, wt, back, fill, load_sem, own_sem, send_sem, recv_sem,
):
    me = lax.axis_index("col")
    sd, cd, width = toks.shape[1:]
    cols = n * cd
    head = width // HEADS
    total = sd * cols

    barrier = pltpu.get_barrier_semaphore()

    def peer(k):
        return lax.rem(me + k, n)

    def greet(k):
        pl.semaphore_signal(barrier, inc=1, device_id={"col": peer(k + 1)}, device_id_type=MESH)

    each(n - 1, greet)
    loads = []
    for k, w in enumerate((wq, wk, wv, wo)):
        loads.append(pltpu.make_async_copy(w, ws.at[k], load_sem.at[k]))
    loads.append(pltpu.make_async_copy(gain, gb, load_sem.at[4]))
    loads.append(pltpu.make_async_copy(bias, bb, load_sem.at[5]))
    own_in = pltpu.make_async_copy(x.at[pl.ds(me * sd, sd)], toks.at[me], own_sem.at[0])
    pl.semaphore_wait(barrier, n - 1)

    def remote(src, dst, phase, p):
        pltpu.make_async_remote_copy(
            src_ref=src, dst_ref=dst, send_sem=send_sem.at[phase], recv_sem=recv_sem.at[phase],
            device_id={"col": p}, device_id_type=MESH,
        ).start()

    def send_tokens(k):
        p = peer(k + 1)
        remote(x.at[pl.ds(p * sd, sd)], toks.at[me], 0, p)

    each(n - 1, send_tokens)
    own_in.start()
    for k in (4, 5, 0, 1, 2, 3):
        loads[k].start()
    loads[4].wait()
    loads[5].wait()
    gain_f = gb[...].astype(jnp.float32).reshape(1, width)
    bias_f = bb[...].astype(jnp.float32).reshape(1, width)
    own_in.wait()
    others = pl.ds(0, n - 1)
    drain(toks.at[others], recv_sem.at[0])

    for s in range(sd):
        gather_rows(
            n, cd, lambda p: toks[p, s].astype(jnp.float32), rows.at[pl.ds(s * cols, cols)]
        )
    a = rows[...]
    center = jnp.sum(a, axis=-1, keepdims=True) * (1.0 / width)
    shifted = a - center
    spread = jnp.sum(shifted * shifted, axis=-1, keepdims=True) * (1.0 / width)
    normed = (shifted * lax.rsqrt(spread + 1e-05) * gain_f + bias_f).astype(jnp.bfloat16)

    def project(k, factor):
        product = jnp.dot(normed, ws[k], preferred_element_type=jnp.float32)
        return (product * factor if factor != 1.0 else product).astype(jnp.bfloat16)

    group = 4
    wide = group * head
    lane = lax.broadcasted_iota(jnp.int32, (cols, wide), 1)

    def spread_heads(block):
        zero = jnp.zeros_like(block)
        return jnp.concatenate(
            [
                jnp.where((lane >= h * head) & (lane < (h + 1) * head), block, zero)
                for h in range(group)
            ],
            axis=0,
        )

    loads[0].wait()
    queries = project(0, 1.0 / math.sqrt(head * sd * n))
    loads[1].wait()
    keys = project(1, 1.0)
    for g in range(HEADS // group):
        f = slice(g * wide, (g + 1) * wide)
        acc = None
        for s in range(sd):
            r = slice(s * cols, (s + 1) * cols)
            part = lax.dot_general(
                queries[r, f], spread_heads(keys[r, f]), (((1,), (1,)), ((), ())),
                preferred_element_type=jnp.float32,
            )
            acc = part if acc is None else acc + part
        lg[:, g * group * cols : (g + 1) * group * cols] = acc

    def pack_logits(p, block):
        lg_send[p] = block

    scatter_rows(n, cd, lg, pack_logits)
    lg_recv[me] = lg_send[me]

    def send_logits(k):
        p = peer(k + 1)
        remote(lg_send.at[p], lg_recv.at[me], 1, p)

    each(n - 1, send_logits)

    loads[2].wait()
    vals = project(2, 1.0)

    drain(lg_recv.at[others], recv_sem.at[1])
    span = max(cols, 128)
    per = span // cols
    seg = lax.broadcasted_iota(jnp.int32, (cd, span), 1)
    for c in range(HEADS // per):
        part = slice(c * span, (c + 1) * span)
        if n <= 16:
            logits = lg_recv[0, :, part]
            for p in range(1, n):
                logits = logits + lg_recv[p, :, part]
        else:
            logits = lax.fori_loop(
                1, n, lambda p, t: t + lg_recv[p, :, part], lg_recv[0, :, part]
            )
        inside = [(seg >= k * cols) & (seg < (k + 1) * cols) for k in range(per)]
        highest = jnp.zeros_like(logits)
        for m in inside:
            top = jnp.max(jnp.where(m, logits, -jnp.inf), axis=-1, keepdims=True)
            highest = jnp.where(m, top, highest)
        expo = jnp.exp(logits - highest)
        norm = jnp.zeros_like(logits)
        for m in inside:
            norm = jnp.where(m, jnp.sum(jnp.where(m, expo, 0.0), axis=-1, keepdims=True), norm)
        wt_all[me, :, part] = (expo / norm).astype(jnp.bfloat16)

    def send_weights(k):
        remote(wt_all.at[me], wt_all.at[me], 2, peer(k + 1))

    each(n - 1, send_weights)
    loads[3].wait()
    drain(wt_all.at[others], recv_sem.at[2])

    gather_rows(n, cd, lambda p: wt_all[p].astype(jnp.float32), wt)
    weights = wt[...].astype(jnp.bfloat16)
    blocks = []
    for s in range(sd):
        r = slice(s * cols, (s + 1) * cols)
        line = []
        for g in range(HEADS // group):
            line.append(
                jnp.dot(
                    weights[:, g * group * cols : (g + 1) * group * cols],
                    spread_heads(vals[r, g * wide : (g + 1) * wide]),
                    preferred_element_type=jnp.float32,
                ).astype(jnp.bfloat16)
            )
        blocks.append(jnp.concatenate(line, axis=1))
    mixed = jnp.concatenate(blocks, axis=0)
    fill[...] = jnp.dot(mixed, ws[3], preferred_element_type=jnp.float32)

    for s in range(sd):

        def pack_back(p, block):
            back[p, s] = block.astype(jnp.bfloat16)

        scatter_rows(n, cd, fill.at[pl.ds(s * cols, cols)], pack_back)

    def send_back(k):
        p = peer(k + 1)
        remote(back.at[p], out.at[pl.ds(me * sd, sd)], 3, p)

    each(n - 1, send_back)
    own_out = pltpu.make_async_copy(back.at[me], out.at[pl.ds(me * sd, sd)], own_sem.at[1])
    own_out.start()
    drain(toks.at[others], send_sem.at[0])
    drain(lg_send.at[others], send_sem.at[1])
    drain(wt_all.at[others], send_sem.at[2])
    drain(back.at[others], send_sem.at[3])
    own_out.wait()
    drain(out.at[pl.ds(0, sd * (n - 1))], recv_sem.at[3])


def local(n, x, *params):
    seqs, cd, width = x.shape
    sd = seqs // n
    cols = n * cd
    bf, f32 = jnp.bfloat16, jnp.float32
    tokens = sd * cols
    anywhere = pl.BlockSpec(memory_space=pl.ANY)
    return pl.pallas_call(
        functools.partial(kernel, n),
        out_shape=jax.ShapeDtypeStruct(x.shape, bf),
        in_specs=[anywhere] * 7,
        out_specs=anywhere,
        scratch_shapes=[
            pltpu.VMEM((n, sd, cd, width), bf),
            pltpu.VMEM((tokens, width), f32),
            pltpu.VMEM((width,), bf),
            pltpu.VMEM((width,), bf),
            pltpu.VMEM((4, width, width), bf),
            pltpu.VMEM((cols, HEADS * cols), f32),
            pltpu.VMEM((n, cd, HEADS * cols), f32),
            pltpu.VMEM((n, cd, HEADS * cols), f32),
            pltpu.VMEM((n, cd, HEADS * cols), bf),
            pltpu.VMEM((cols, HEADS * cols), f32),
            pltpu.VMEM((n, sd, cd, width), bf),
            pltpu.VMEM((tokens, width), f32),
            pltpu.SemaphoreType.DMA((6,)),
            pltpu.SemaphoreType.DMA((2,)),
            pltpu.SemaphoreType.DMA((4,)),
            pltpu.SemaphoreType.DMA((4,)),
        ],
        compiler_params=pltpu.CompilerParams(
            collective_id=0, has_side_effects=True, vmem_limit_bytes=56 * 2**20
        ),
    )(x, *params)


def solution(mesh):
    placed = (P("rep", "col", None), P(), P(), P(), P(), P(), P())
    return jax.shard_map(
        functools.partial(local, mesh.shape["col"]),
        mesh=mesh, in_specs=placed, out_specs=P("rep", "col", None), check_vma=False,
    )
```

```python
import functools
import math

import jax
import jax.numpy as jnp
from jax import lax
from jax.experimental import pallas as pl
from jax.experimental.pallas import tpu as pltpu
from jax.sharding import PartitionSpec as P

HEADS = 12
MESH = pl.DeviceIdType.MESH


def each(count, body):
    if count <= 16:
        for k in range(count):
            body(k)
    else:
        lax.fori_loop(0, count, lambda k, c: (body(k), c)[1], 0)


def around(n, body):
    def pair(k):
        body(k + 1)
        body(n - 1 - k)

    each((n - 1) // 2, pair)
    if n % 2 == 0:
        body(n // 2)


def scatter_rows(n, cd, source, put):
    if n <= 16:
        for p in range(n):
            put(p, source[p * cd : (p + 1) * cd, :])
        return
    per = max(8 // cd, 1)

    def body(q):
        tile = source[pl.ds(pl.multiple_of(q * per * cd, per * cd), per * cd), :]
        for k in range(per):
            put(q * per + k, tile[k * cd : (k + 1) * cd, :])

    each(n // per, body)


def gather_rows(n, cd, take, target):
    if n <= 16:
        for p in range(n):
            target[p * cd : (p + 1) * cd, :] = take(p)
        return
    per = max(8 // cd, 1)

    def body(q):
        tile = jnp.concatenate([take(q * per + k) for k in range(per)], axis=0)
        target[pl.ds(pl.multiple_of(q * per * cd, per * cd), per * cd), :] = tile

    each(n // per, body)


def drain(like, sem):
    pltpu.make_async_copy(like, like, sem).wait()


def kernel(
    n, x, gain, bias, wq, wk, wv, wo, out,
    toks, stage, rows, gb, bb, ws, lg, lg_send, lg_recv, wt_all, wt, back, fill, load_sem, own_sem, send_sem, recv_sem,
):
    me = lax.axis_index("col")
    sd, cd, width = toks.shape[1:]
    cols = n * cd
    head = width // HEADS
    total = sd * cols

    barrier = pltpu.get_barrier_semaphore()

    def peer(k):
        return lax.rem(me + k, n)

    def greet(k):
        pl.semaphore_signal(barrier, inc=1, device_id={"col": peer(k + 1)}, device_id_type=MESH)

    each(n - 1, greet)
    loads = []
    for k, w in enumerate((wq, wk, wv, wo)):
        loads.append(pltpu.make_async_copy(w, ws.at[k], load_sem.at[k]))
    loads.append(pltpu.make_async_copy(gain, gb, load_sem.at[4]))
    loads.append(pltpu.make_async_copy(bias, bb, load_sem.at[5]))
    staged = pltpu.make_async_copy(x, stage, own_sem.at[0])
    staged.start()
    for k in (0, 1, 4, 5, 2, 3):
        loads[k].start()
    pl.semaphore_wait(barrier, n - 1)

    def remote(src, dst, phase, p):
        pltpu.make_async_remote_copy(
            src_ref=src, dst_ref=dst, send_sem=send_sem.at[phase], recv_sem=recv_sem.at[phase],
            device_id={"col": p}, device_id_type=MESH,
        ).start()

    staged.wait()

    def send_tokens(k):
        p = peer(k)
        remote(stage.at[pl.ds(p * sd, sd)], toks.at[me], 0, p)

    around(n, send_tokens)
    toks[me] = stage[pl.ds(me * sd, sd)]
    loads[4].wait()
    loads[5].wait()
    gain_f = gb[...].astype(jnp.float32).reshape(1, width)
    bias_f = bb[...].astype(jnp.float32).reshape(1, width)
    others = pl.ds(0, n - 1)
    drain(toks.at[others], recv_sem.at[0])

    for s in range(sd):
        gather_rows(
            n, cd, lambda p: toks[p, s].astype(jnp.float32), rows.at[pl.ds(s * cols, cols)]
        )
    a = rows[...]
    center = jnp.sum(a, axis=-1, keepdims=True) * (1.0 / width)
    shifted = a - center
    spread = jnp.sum(shifted * shifted, axis=-1, keepdims=True) * (1.0 / width)
    normed = (shifted * lax.rsqrt(spread + 1e-05) * gain_f + bias_f).astype(jnp.bfloat16)

    def project(k, factor):
        product = jnp.dot(normed, ws[k], preferred_element_type=jnp.float32)
        return (product * factor if factor != 1.0 else product).astype(jnp.bfloat16)

    group = 4
    wide = group * head
    lane = lax.broadcasted_iota(jnp.int32, (cols, wide), 1)

    def spread_heads(block):
        zero = jnp.zeros_like(block)
        return jnp.concatenate(
            [
                jnp.where((lane >= h * head) & (lane < (h + 1) * head), block, zero)
                for h in range(group)
            ],
            axis=0,
        )

    loads[0].wait()
    queries = project(0, 1.0 / math.sqrt(head * sd * n))
    loads[1].wait()
    keys = project(1, 1.0)
    for g in range(HEADS // group):
        f = slice(g * wide, (g + 1) * wide)
        acc = None
        for s in range(sd):
            r = slice(s * cols, (s + 1) * cols)
            part = lax.dot_general(
                queries[r, f], spread_heads(keys[r, f]), (((1,), (1,)), ((), ())),
                preferred_element_type=jnp.float32,
            )
            acc = part if acc is None else acc + part
        lg[:, g * group * cols : (g + 1) * group * cols] = acc

    def pack_logits(p, block):
        lg_send[p] = block

    scatter_rows(n, cd, lg, pack_logits)
    lg_recv[me] = lg_send[me]

    def send_logits(k):
        p = peer(k)
        remote(lg_send.at[p], lg_recv.at[me], 1, p)

    around(n, send_logits)

    loads[2].wait()
    vals = project(2, 1.0)

    drain(lg_recv.at[others], recv_sem.at[1])
    span = max(cols, 128)
    per = span // cols
    seg = lax.broadcasted_iota(jnp.int32, (cd, span), 1)
    for c in range(HEADS // per):
        part = slice(c * span, (c + 1) * span)
        if n <= 16:
            logits = lg_recv[0, :, part]
            for p in range(1, n):
                logits = logits + lg_recv[p, :, part]
        else:
            logits = lax.fori_loop(
                1, n, lambda p, t: t + lg_recv[p, :, part], lg_recv[0, :, part]
            )
        inside = [(seg >= k * cols) & (seg < (k + 1) * cols) for k in range(per)]
        highest = jnp.zeros_like(logits)
        for m in inside:
            top = jnp.max(jnp.where(m, logits, -jnp.inf), axis=-1, keepdims=True)
            highest = jnp.where(m, top, highest)
        expo = jnp.exp(logits - highest)
        norm = jnp.zeros_like(logits)
        for m in inside:
            norm = jnp.where(m, jnp.sum(jnp.where(m, expo, 0.0), axis=-1, keepdims=True), norm)
        wt_all[me, :, part] = (expo / norm).astype(jnp.bfloat16)

    def send_weights(k):
        remote(wt_all.at[me], wt_all.at[me], 2, peer(k))

    around(n, send_weights)
    loads[3].wait()
    drain(wt_all.at[others], recv_sem.at[2])

    gather_rows(n, cd, lambda p: wt_all[p].astype(jnp.float32), wt)
    weights = wt[...].astype(jnp.bfloat16)
    blocks = []
    for s in range(sd):
        r = slice(s * cols, (s + 1) * cols)
        line = []
        for g in range(HEADS // group):
            line.append(
                jnp.dot(
                    weights[:, g * group * cols : (g + 1) * group * cols],
                    spread_heads(vals[r, g * wide : (g + 1) * wide]),
                    preferred_element_type=jnp.float32,
                ).astype(jnp.bfloat16)
            )
        blocks.append(jnp.concatenate(line, axis=1))
    mixed = jnp.concatenate(blocks, axis=0)
    fill[...] = jnp.dot(mixed, ws[3], preferred_element_type=jnp.float32)

    for s in range(sd):

        def pack_back(p, block):
            back[p, s] = block.astype(jnp.bfloat16)

        scatter_rows(n, cd, fill.at[pl.ds(s * cols, cols)], pack_back)

    def send_back(k):
        p = peer(k)
        remote(back.at[p], out.at[pl.ds(me * sd, sd)], 3, p)

    around(n, send_back)
    own_out = pltpu.make_async_copy(back.at[me], out.at[pl.ds(me * sd, sd)], own_sem.at[1])
    own_out.start()
    drain(toks.at[others], send_sem.at[0])
    drain(lg_send.at[others], send_sem.at[1])
    drain(wt_all.at[others], send_sem.at[2])
    drain(back.at[others], send_sem.at[3])
    own_out.wait()
    drain(out.at[pl.ds(0, sd * (n - 1))], recv_sem.at[3])


def local(n, x, *params):
    seqs, cd, width = x.shape
    sd = seqs // n
    cols = n * cd
    bf, f32 = jnp.bfloat16, jnp.float32
    tokens = sd * cols
    anywhere = pl.BlockSpec(memory_space=pl.ANY)
    return pl.pallas_call(
        functools.partial(kernel, n),
        out_shape=pltpu.VMEM(x.shape, bf),
        in_specs=[anywhere] * 7,
        out_specs=pl.BlockSpec(memory_space=pltpu.VMEM),
        scratch_shapes=[
            pltpu.VMEM((n, sd, cd, width), bf),
            pltpu.VMEM(x.shape, bf),
            pltpu.VMEM((tokens, width), f32),
            pltpu.VMEM((width,), bf),
            pltpu.VMEM((width,), bf),
            pltpu.VMEM((4, width, width), bf),
            pltpu.VMEM((cols, HEADS * cols), f32),
            pltpu.VMEM((n, cd, HEADS * cols), f32),
            pltpu.VMEM((n, cd, HEADS * cols), f32),
            pltpu.VMEM((n, cd, HEADS * cols), bf),
            pltpu.VMEM((cols, HEADS * cols), f32),
            pltpu.VMEM((n, sd, cd, width), bf),
            pltpu.VMEM((tokens, width), f32),
            pltpu.SemaphoreType.DMA((6,)),
            pltpu.SemaphoreType.DMA((2,)),
            pltpu.SemaphoreType.DMA((4,)),
            pltpu.SemaphoreType.DMA((4,)),
        ],
        compiler_params=pltpu.CompilerParams(
            collective_id=0, has_side_effects=True, vmem_limit_bytes=56 * 2**20
        ),
    )(x, *params)


def solution(mesh):
    placed = (P("rep", "col", None), P(), P(), P(), P(), P(), P())
    return jax.shard_map(
        functools.partial(local, mesh.shape["col"]),
        mesh=mesh, in_specs=placed, out_specs=P("rep", "col", None), check_vma=False,
    )
```

```python
import functools
import math

import jax
import jax.numpy as jnp
from jax import lax
from jax.experimental import pallas as pl
from jax.experimental.pallas import tpu as pltpu
from jax.sharding import PartitionSpec as P

HEADS = 12
MESH = pl.DeviceIdType.MESH


def each(count, body):
    if count <= 16:
        for k in range(count):
            body(k)
    else:
        lax.fori_loop(0, count, lambda k, c: (body(k), c)[1], 0)


def around(n, body):
    def pair(k):
        body(k + 1)
        body(n - 1 - k)

    each((n - 1) // 2, pair)
    if n % 2 == 0:
        body(n // 2)


def scatter_rows(n, cd, source, put):
    if n <= 16:
        for p in range(n):
            put(p, source[p * cd : (p + 1) * cd, :])
        return
    per = max(8 // cd, 1)

    def body(q):
        tile = source[pl.ds(pl.multiple_of(q * per * cd, per * cd), per * cd), :]
        for k in range(per):
            put(q * per + k, tile[k * cd : (k + 1) * cd, :])

    each(n // per, body)


def gather_rows(n, cd, take, target):
    if n <= 16:
        for p in range(n):
            target[p * cd : (p + 1) * cd, :] = take(p)
        return
    per = max(8 // cd, 1)

    def body(q):
        tile = jnp.concatenate([take(q * per + k) for k in range(per)], axis=0)
        target[pl.ds(pl.multiple_of(q * per * cd, per * cd), per * cd), :] = tile

    each(n // per, body)


def drain(like, sem):
    pltpu.make_async_copy(like, like, sem).wait()


def kernel(
    n, x, gain, bias, wq, wk, wv, wo, out,
    toks, stage, rows, gb, bb, ws, lg, lg_send, lg_recv, wt_all, wt, back, fill, load_sem, own_sem, send_sem, recv_sem,
):
    me = lax.axis_index("col")
    sd, cd, width = toks.shape[1:]
    cols = n * cd
    head = width // HEADS
    total = sd * cols

    barrier = pltpu.get_barrier_semaphore()

    def peer(k):
        return lax.rem(me + k, n)

    def greet(k):
        pl.semaphore_signal(barrier, inc=1, device_id={"col": peer(k + 1)}, device_id_type=MESH)

    each(n - 1, greet)
    loads = []
    for k, w in enumerate((wq, wk, wv, wo)):
        loads.append(pltpu.make_async_copy(w, ws.at[k], load_sem.at[k]))
    loads.append(pltpu.make_async_copy(gain, gb, load_sem.at[4]))
    loads.append(pltpu.make_async_copy(bias, bb, load_sem.at[5]))
    staged = pltpu.make_async_copy(x, stage, own_sem.at[0])
    staged.start()
    for k in (4, 5, 0, 1, 2, 3):
        loads[k].start()
    loads[4].wait()
    loads[5].wait()
    gain_f = gb[...].astype(jnp.float32).reshape(1, 1, width)
    bias_f = bb[...].astype(jnp.float32).reshape(1, 1, width)
    staged.wait()

    def normalize(p):
        block = pl.ds(p * sd, sd)
        a = stage[block].astype(jnp.float32)
        center = jnp.sum(a, axis=-1, keepdims=True) * (1.0 / width)
        shifted = a - center
        spread = jnp.sum(shifted * shifted, axis=-1, keepdims=True) * (1.0 / width)
        stage[block] = (shifted * lax.rsqrt(spread + 1e-05) * gain_f + bias_f).astype(jnp.bfloat16)

    each(n, normalize)
    pl.semaphore_wait(barrier, n - 1)

    def remote(src, dst, phase, p):
        pltpu.make_async_remote_copy(
            src_ref=src, dst_ref=dst, send_sem=send_sem.at[phase], recv_sem=recv_sem.at[phase],
            device_id={"col": p}, device_id_type=MESH,
        ).start()

    def send_tokens(k):
        p = peer(k)
        remote(stage.at[pl.ds(p * sd, sd)], toks.at[me], 0, p)

    around(n, send_tokens)
    toks[me] = stage[pl.ds(me * sd, sd)]
    others = pl.ds(0, n - 1)
    drain(toks.at[others], recv_sem.at[0])

    for s in range(sd):
        gather_rows(
            n, cd, lambda p: toks[p, s].astype(jnp.float32), rows.at[pl.ds(s * cols, cols)]
        )
    normed = rows[...].astype(jnp.bfloat16)

    def project(k, factor):
        product = jnp.dot(normed, ws[k], preferred_element_type=jnp.float32)
        return (product * factor if factor != 1.0 else product).astype(jnp.bfloat16)

    group = 4
    wide = group * head
    lane = lax.broadcasted_iota(jnp.int32, (cols, wide), 1)

    def spread_heads(block):
        zero = jnp.zeros_like(block)
        return jnp.concatenate(
            [
                jnp.where((lane >= h * head) & (lane < (h + 1) * head), block, zero)
                for h in range(group)
            ],
            axis=0,
        )

    loads[0].wait()
    queries = project(0, 1.0 / math.sqrt(head * sd * n))
    loads[1].wait()
    keys = project(1, 1.0)
    for g in range(HEADS // group):
        f = slice(g * wide, (g + 1) * wide)
        acc = None
        for s in range(sd):
            r = slice(s * cols, (s + 1) * cols)
            part = lax.dot_general(
                queries[r, f], spread_heads(keys[r, f]), (((1,), (1,)), ((), ())),
                preferred_element_type=jnp.float32,
            )
            acc = part if acc is None else acc + part
        lg[:, g * group * cols : (g + 1) * group * cols] = acc

    def pack_logits(p, block):
        lg_send[p] = block

    scatter_rows(n, cd, lg, pack_logits)
    lg_recv[me] = lg_send[me]

    def send_logits(k):
        p = peer(k)
        remote(lg_send.at[p], lg_recv.at[me], 1, p)

    around(n, send_logits)

    loads[2].wait()
    vals = project(2, 1.0)

    drain(lg_recv.at[others], recv_sem.at[1])
    span = max(cols, 128)
    per = span // cols
    seg = lax.broadcasted_iota(jnp.int32, (cd, span), 1)
    for c in range(HEADS // per):
        part = slice(c * span, (c + 1) * span)
        if n <= 16:
            logits = lg_recv[0, :, part]
            for p in range(1, n):
                logits = logits + lg_recv[p, :, part]
        else:
            logits = lax.fori_loop(
                1, n, lambda p, t: t + lg_recv[p, :, part], lg_recv[0, :, part]
            )
        inside = [(seg >= k * cols) & (seg < (k + 1) * cols) for k in range(per)]
        highest = jnp.zeros_like(logits)
        for m in inside:
            top = jnp.max(jnp.where(m, logits, -jnp.inf), axis=-1, keepdims=True)
            highest = jnp.where(m, top, highest)
        expo = jnp.exp(logits - highest)
        norm = jnp.zeros_like(logits)
        for m in inside:
            norm = jnp.where(m, jnp.sum(jnp.where(m, expo, 0.0), axis=-1, keepdims=True), norm)
        wt_all[me, :, part] = (expo / norm).astype(jnp.bfloat16)

    def send_weights(k):
        remote(wt_all.at[me], wt_all.at[me], 2, peer(k))

    around(n, send_weights)
    loads[3].wait()
    drain(wt_all.at[others], recv_sem.at[2])

    gather_rows(n, cd, lambda p: wt_all[p].astype(jnp.float32), wt)
    weights = wt[...].astype(jnp.bfloat16)
    blocks = []
    for s in range(sd):
        r = slice(s * cols, (s + 1) * cols)
        line = []
        for g in range(HEADS // group):
            line.append(
                jnp.dot(
                    weights[:, g * group * cols : (g + 1) * group * cols],
                    spread_heads(vals[r, g * wide : (g + 1) * wide]),
                    preferred_element_type=jnp.float32,
                ).astype(jnp.bfloat16)
            )
        blocks.append(jnp.concatenate(line, axis=1))
    mixed = jnp.concatenate(blocks, axis=0)
    fill[...] = jnp.dot(mixed, ws[3], preferred_element_type=jnp.float32)

    for s in range(sd):

        def pack_back(p, block):
            back[p, s] = block.astype(jnp.bfloat16)

        scatter_rows(n, cd, fill.at[pl.ds(s * cols, cols)], pack_back)

    def send_back(k):
        p = peer(k)
        remote(back.at[p], out.at[pl.ds(me * sd, sd)], 3, p)

    around(n, send_back)
    own_out = pltpu.make_async_copy(back.at[me], out.at[pl.ds(me * sd, sd)], own_sem.at[1])
    own_out.start()
    drain(toks.at[others], send_sem.at[0])
    drain(lg_send.at[others], send_sem.at[1])
    drain(wt_all.at[others], send_sem.at[2])
    drain(back.at[others], send_sem.at[3])
    own_out.wait()
    drain(out.at[pl.ds(0, sd * (n - 1))], recv_sem.at[3])


def local(n, x, *params):
    seqs, cd, width = x.shape
    sd = seqs // n
    cols = n * cd
    bf, f32 = jnp.bfloat16, jnp.float32
    tokens = sd * cols
    anywhere = pl.BlockSpec(memory_space=pl.ANY)
    return pl.pallas_call(
        functools.partial(kernel, n),
        out_shape=pltpu.VMEM(x.shape, bf),
        in_specs=[anywhere] * 7,
        out_specs=pl.BlockSpec(memory_space=pltpu.VMEM),
        scratch_shapes=[
            pltpu.VMEM((n, sd, cd, width), bf),
            pltpu.VMEM(x.shape, bf),
            pltpu.VMEM((tokens, width), f32),
            pltpu.VMEM((width,), bf),
            pltpu.VMEM((width,), bf),
            pltpu.VMEM((4, width, width), bf),
            pltpu.VMEM((cols, HEADS * cols), f32),
            pltpu.VMEM((n, cd, HEADS * cols), f32),
            pltpu.VMEM((n, cd, HEADS * cols), f32),
            pltpu.VMEM((n, cd, HEADS * cols), bf),
            pltpu.VMEM((cols, HEADS * cols), f32),
            pltpu.VMEM((n, sd, cd, width), bf),
            pltpu.VMEM((tokens, width), f32),
            pltpu.SemaphoreType.DMA((6,)),
            pltpu.SemaphoreType.DMA((2,)),
            pltpu.SemaphoreType.DMA((4,)),
            pltpu.SemaphoreType.DMA((4,)),
        ],
        compiler_params=pltpu.CompilerParams(
            collective_id=0, has_side_effects=True, vmem_limit_bytes=56 * 2**20
        ),
    )(x, *params)


def solution(mesh):
    placed = (P("rep", "col", None), P(), P(), P(), P(), P(), P())
    return jax.shard_map(
        functools.partial(local, mesh.shape["col"]),
        mesh=mesh, in_specs=placed, out_specs=P("rep", "col", None), check_vma=False,
    )
```
